256 devices in a mesh: row: 8 (over x, y_hi), col: 32 (over y_lo, z, core).
Axes of the slice: x: 4, y: 4 (y_hi: 2, y_lo: 2; y = y_hi * 2 + y_lo), z: 8, core: 2. Of those that a mesh axis runs over, the one named last changes fastest.
Arguments:
- tiles: bfloat16 [12288, 256, 256], P(('row', 'col')), as said below
- tile_row: int32 [12288], P(('row', 'col')), may hold values from 0 to 255, as said below
- tile_col: int32 [12288], P(('row', 'col')), may hold values from 0 to 255, as said below
- label_class: int32 [65536], P(('row', 'col')), may hold values from -1 to 127, as said below
Outputs:
- scores: float32 [65536, 128], P(('row', 'col'))
- residual: float32 [65536, 128], P(('row', 'col'))
The draws below stay inside these ranges and needn't reach their ends.
Inputs may be any that keep to these rules, and one draw needn't show every extreme that they name: `tiles`: Nonnegative. The tile of blocks (j, i) is the transpose of the tile of blocks (i, j); a tile on the diagonal is symmetric. No pair of blocks appears twice; the pair (j, i) is stored whenever (i, j) is. The device with row index r and col index c holds 48 tiles, all with tile_row // 32 == r and tile_col % 32 == c. `tile_col`: see tile_row. `label_class`: exactly 8192 nodes are labeled, and every class labels at least one node.
All inputs are finite; a program needn't handle non-finite values.
Results may differ from the reference program's by a relative error of at most 0.00062.
Values may be sent and summed in bfloat16 or wider, within the bound.
No kernel may reach another device: no remote copies, remote signals or barrier semaphores. Data moves between devices by JAX's collectives and lax.ppermute only.
A program may use at most 64 MiB of HBM per device.

```python
import jax
import jax.numpy as jnp
from jax import lax

TILE = 256
CLASSES = 128
ITERS = 3
BLOCKS = 256
TILES_DEV = 48
NODES = 65536
N_COL = 32


def tile_pattern(key):
    pair_count = (TILES_DEV - 2) // 2
    shuffled = jax.random.permutation(jax.random.fold_in(key, 11), BLOCKS // 2 - 1) + 1
    chosen = shuffled[:pair_count].astype(jnp.int32)
    offsets = jnp.concatenate([jnp.array([0, BLOCKS // 2], jnp.int32), chosen, BLOCKS - chosen]).astype(jnp.int32)
    device = jnp.arange(BLOCKS, dtype=jnp.int32)[:, None]
    row_index = device // N_COL
    col_index = device % N_COL
    col_part = (col_index - offsets[None, :]) % N_COL
    rows = row_index * N_COL + col_part
    cols = (rows + offsets[None, :]) % BLOCKS
    return (rows.reshape(-1).astype(jnp.int32), cols.reshape(-1).astype(jnp.int32))


def draw_tile_row(key, part):
    return tile_pattern(key)[0]


def draw_tile_col(key, part):
    return tile_pattern(key)[1]


def draw_tiles(key, part):
    rows, cols = tile_pattern(key)
    smaller = jnp.minimum(rows, cols)
    larger = jnp.maximum(rows, cols)
    pair_id = smaller * BLOCKS + larger
    scale_value = 400.0 * CLASSES / (TILES_DEV * TILE)

    def one_tile(element):
        pair_value, transposed, on_diagonal = element
        pair_key = jax.random.fold_in(jax.random.fold_in(key, 23), pair_value)
        first_key, second_key = jax.random.split(pair_key)
        entries = jnp.exp(-6.0 * jax.random.uniform(first_key, (TILE, TILE), jnp.float32))
        factor = jnp.exp(jnp.log(0.01) * jax.random.uniform(second_key, (), jnp.float32))
        entries = entries * factor
        entries = jnp.where(on_diagonal, 0.5 * (entries + entries.T), jnp.where(transposed, entries.T, entries))
        return (entries * scale_value).astype(jnp.bfloat16)
    return lax.map(one_tile, (pair_id, rows > cols, rows == cols))


def draw_label_class(key, part):
    shuffled = jax.random.permutation(jax.random.fold_in(key, 5), NODES)
    random_class = jax.random.randint(jax.random.fold_in(key, 6), (NODES,), 0, CLASSES)
    ranking = jnp.arange(NODES, dtype=jnp.int32)
    assigned = jnp.where(ranking < CLASSES, ranking, random_class)
    assigned = jnp.where(ranking < NODES // 8, assigned, -1).astype(jnp.int32)
    return jnp.zeros((NODES,), jnp.int32).at[shuffled].set(assigned)


def setup_inputs(seed: int = 0) -> dict:
    splits = jax.random.split(jax.random.key(seed), 5)
    tiles = draw_tiles(jax.random.fold_in(splits[4], 71), 0)
    tile_row = draw_tile_row(jax.random.fold_in(splits[4], 71), 0)
    tile_col = draw_tile_col(jax.random.fold_in(splits[4], 71), 0)
    label_class = draw_label_class(jax.random.fold_in(splits[4], 71), 0)
    return {"tiles": tiles, "tile_row": tile_row, "tile_col": tile_col, "label_class": label_class}


def weight_apply(tiles, tile_row, tile_col, vector_half):
    source = vector_half.reshape(BLOCKS, TILE, CLASSES).astype(jnp.float32)
    grouped = tiles.reshape(BLOCKS, TILES_DEV, TILE, TILE)
    grouped_rows = tile_row.reshape(BLOCKS, TILES_DEV).astype(jnp.int32)
    grouped_cols = tile_col.reshape(BLOCKS, TILES_DEV).astype(jnp.int32)

    def one_group(running, element):
        tile_block, block_row, block_col = element
        products = jnp.einsum("tab,tbk->tak", tile_block.astype(jnp.float32), source[block_col], precision=lax.Precision.HIGHEST)
        return running.at[block_row].add(products), None

    start = jnp.zeros((BLOCKS, TILE, CLASSES), jnp.float32)
    running, _ = lax.scan(one_group, start, (grouped, grouped_rows, grouped_cols))
    return running.reshape(NODES, CLASSES)


def reference(tiles, tile_row, tile_col, label_class):
    row_sums = jnp.sum(tiles.astype(jnp.float32), axis=2)
    degree = jax.ops.segment_sum(row_sums, tile_row.astype(jnp.int32), num_segments=BLOCKS).reshape(NODES)
    unlabeled = label_class < 0
    onehot = (label_class[:, None] == jnp.arange(CLASSES, dtype=jnp.int32)[None, :]).astype(jnp.bfloat16)
    rhs = jnp.where(unlabeled[:, None], weight_apply(tiles, tile_row, tile_col, onehot), jnp.float32(0.0))

    def operator(direction):
        mixed = weight_apply(tiles, tile_row, tile_col, direction.astype(jnp.bfloat16))
        return jnp.where(unlabeled[:, None], degree[:, None] * direction - mixed, direction)

    solution = jnp.zeros((NODES, CLASSES), jnp.float32)
    residual = rhs
    direction = rhs
    norm_now = jnp.sum(residual * residual, axis=0)
    for iteration in range(ITERS):
        image = operator(direction)
        alpha = norm_now / jnp.sum(direction * image, axis=0)
        solution = solution + alpha * direction
        residual = residual - alpha * image
        norm_next = jnp.sum(residual * residual, axis=0)
        direction = residual + (norm_next / norm_now) * direction
        norm_now = norm_next
    return 8.0 * CLASSES * solution, residual
```

```python
import functools

import jax
import jax.numpy as jnp
from jax import lax
from jax.experimental import pallas as pl
from jax.experimental.pallas import tpu as pltpu
from jax.sharding import Mesh
from jax.sharding import PartitionSpec as P

CLASSES = 128
ITERS = 3
AXES = ("x", "yh", "yl", "z", "core")
ROW = ("x", "yh")
COL = ("yl", "z", "core")
F32 = jnp.float32
BF16 = jnp.bfloat16
CHUNK = 8
PARAMS = pltpu.CompilerParams(vmem_limit_bytes=40 * 1024 * 1024)
VMEM = pl.BlockSpec(memory_space=pltpu.VMEM)
SMEM = pl.BlockSpec(memory_space=pltpu.SMEM)


def shape(dims, dtype=F32):
    return jax.ShapeDtypeStruct(dims, dtype)


def to_everyone(copies, axis):
    return lax.all_to_all(copies, axis, 0, 0, tiled=True)


def shift(array, axis, by):
    size = lax.axis_size(axis)
    return lax.ppermute(array, axis, [(i, (i + by) % size) for i in range(size)])


def accumulate(rows, panel_of, source_ref, target_ref, tiles_ref, parts, total):
    step = pl.program_id(0)

    @pl.when(step == 0)
    def _():
        total[...] = jnp.zeros_like(total)

    for t in range(CHUNK):
        at = step * CHUNK + t
        product = jnp.dot(
            panel_of(source_ref[at]), tiles_ref[t], preferred_element_type=F32
        )
        total[target_ref[at]] += product[:rows]

    @pl.when(step == pl.num_programs(0) - 1)
    def _():
        for k, part in enumerate(parts):
            part[...] = total[2 * k : 2 * k + 2]


def label_kernel(source_ref, target_ref, label_ref, tiles_ref, *rest):
    *parts, total = rest
    size = tiles_ref.shape[1]
    classes = lax.broadcasted_iota(jnp.int32, (CLASSES, size), 0)

    def panel_of(source):
        hot = jnp.where(label_ref[source] == classes, F32(1.0), F32(0.0))
        return jnp.concatenate([hot, jnp.ones((16, size), F32)], axis=0).astype(BF16)

    accumulate(CLASSES + 8, panel_of, source_ref, target_ref, tiles_ref, parts, total)


def panel_kernel(source_ref, target_ref, own_ref, other_ref, tiles_ref, *rest):
    *parts, total = rest
    half = own_ref.shape[0]

    def panel_of(source):
        at = lax.rem(source, half)
        return jnp.where(source < half, own_ref[at], other_ref[at])

    accumulate(CLASSES, panel_of, source_ref, target_ref, tiles_ref, parts, total)


def apply_tiles(kernel, rows, source, target, tiles, *panels):
    count, size, _ = tiles.shape
    whole = [pl.BlockSpec(p.shape, lambda g, n=p.ndim: (0,) * n) for p in panels]
    part = shape((2, rows, size))
    return pl.pallas_call(
        kernel,
        grid=(count // CHUNK,),
        in_specs=[SMEM, SMEM, *whole, pl.BlockSpec((CHUNK, size, size), lambda g: (g, 0, 0))],
        out_specs=[pl.BlockSpec(part.shape, lambda g: (0, 0, 0))] * 4,
        out_shape=[part] * 4,
        scratch_shapes=[pltpu.VMEM((8, rows, size), F32)],
        compiler_params=PARAMS,
    )(source, target, *panels, tiles)


def second_kernel(a_ref, b_ref, c_ref, d_ref, out_ref):
    out_ref[...] = (a_ref[1] + b_ref[1]) + (c_ref[1] + d_ref[1])


def reduce_parts(parts):
    arrived = [parts[0], *(shift(parts[k], "x", k) for k in range(1, 4))]
    second = pl.pallas_call(
        second_kernel,
        in_specs=[VMEM] * 4,
        out_specs=VMEM,
        out_shape=shape(parts[0].shape[1:]),
        compiler_params=PARAMS,
    )(*arrived)
    return (*arrived, shift(second, "yh", 1))


def sums_to_rows(sums):
    size = sums[0].shape[0]
    lane = lax.broadcasted_iota(jnp.int32, (size, CLASSES), 1)
    table = jnp.zeros((size, CLASSES), F32)
    for i, column in enumerate(sums):
        table = jnp.where(lane == i, column, table)
    return table.T[:8]


def rows_to_columns(row):
    return jnp.broadcast_to(row, (CLASSES, CLASSES)).T[:, :1]


def merged(a_ref, b_ref, c_ref, d_ref, e_ref):
    return (a_ref[0] + b_ref[0]) + (c_ref[0] + d_ref[0]) + e_ref[...]


def start_kernel(a_ref, b_ref, c_ref, d_ref, e_ref, label_ref, rhs_ref, panel_ref, degree_ref):
    mixed = merged(a_ref, b_ref, c_ref, d_ref, e_ref)
    rhs = jnp.where(label_ref[...] < 0, mixed[:CLASSES], F32(0.0))
    rhs_ref[...] = rhs
    panel_ref[...] = rhs.astype(BF16)
    degree_ref[...] = mixed[CLASSES : CLASSES + 1]


def image_kernel(
    a_ref, b_ref, c_ref, d_ref, e_ref, label_ref, degree_ref, direction_ref, residual_ref,
    image_ref, sums_ref,
):
    mixed = merged(a_ref, b_ref, c_ref, d_ref, e_ref)
    direction = direction_ref[...]
    residual = residual_ref[...]
    image = jnp.where(label_ref[...] < 0, degree_ref[...] * direction - mixed, direction)
    image_ref[...] = image
    rows = sums_to_rows(
        [
            jnp.sum(term, axis=1, keepdims=True)
            for term in (direction * image, residual * image, image * image, residual * residual)
        ]
    )
    for i in range(sums_ref.shape[0]):
        sums_ref[i] = rows


def relay_kernel(in_ref, out_ref):
    rows = jnp.sum(in_ref[...], axis=0)
    for i in range(out_ref.shape[0]):
        out_ref[i] = rows


def step_kernel(
    first, sums_ref, norm_ref, solution_ref, residual_ref, direction_ref, image_ref,
    solution_out, residual_out, direction_out, panel_out, norm_out,
):
    sums = jnp.sum(sums_ref[...], axis=0)
    bending, crossed, energy = sums[0:1], sums[1:2], sums[2:3]
    norm = sums[3:4] if first else norm_ref[...]
    alpha = norm / bending
    norm_next = norm - 2.0 * alpha * crossed + alpha * alpha * energy
    norm_out[...] = norm_next
    beta = rows_to_columns(norm_next / norm)
    alpha = rows_to_columns(alpha)
    direction = direction_ref[...]
    step = alpha * direction
    solution_out[...] = step if first else solution_ref[...] + step
    residual = residual_ref[...] - alpha * image_ref[...]
    residual_out[...] = residual
    direction = residual + beta * direction
    direction_out[...] = direction
    panel_out[...] = direction.astype(BF16)


def last_kernel(
    sums_ref, norm_ref, solution_ref, residual_ref, direction_ref, image_ref,
    scores_out, residual_out,
):
    sums = jnp.sum(sums_ref[...], axis=0)
    alpha = rows_to_columns(norm_ref[...] / sums[0:1])
    total = solution_ref[...] + alpha * direction_ref[...]
    scores_out[...] = (8.0 * CLASSES * total).T
    residual_out[...] = (residual_ref[...] - alpha * image_ref[...]).T


def call(kernel, out_shape, *args):
    return pl.pallas_call(
        kernel,
        in_specs=[VMEM] * len(args),
        out_specs=jax.tree.map(lambda _: VMEM, out_shape),
        out_shape=out_shape,
        compiler_params=PARAMS,
    )(*args)


def gather_panels(panel):
    own = lax.all_gather(panel, "z")
    own = lax.all_gather(own, "yl")
    own = own.reshape(-1, *panel.shape)
    return own, shift(own, "core", 1)


def shards(tiles, tile_row, tile_col, label_class):
    size = tiles.shape[1]
    rows = lax.axis_size(ROW)
    cols = lax.axis_size(COL)
    wide = cols // 2
    local = tile_row % cols
    mine = local % 2 == lax.axis_index("core")
    source = local // 2 + jnp.where(mine, 0, wide)
    block = tile_col // cols
    to_x = (block // 2 - lax.axis_index("x")) % 4
    to_y = (block % 2 - lax.axis_index("yh")) % 2
    target = to_x * 2 + to_y
    label = label_class.reshape(1, size)
    labels = to_everyone(jnp.broadcast_to(label[None], (cols, 1, size)), COL)
    parts = apply_tiles(label_kernel, CLASSES + 8, local, target, tiles, labels)
    field = shape((CLASSES, size))
    half = shape((CLASSES, size), BF16)
    residual, panel, degree = call(
        start_kernel, (field, half, shape((1, size))), *reduce_parts(parts), label
    )
    direction = residual
    solution = residual
    norm = jnp.zeros((1, CLASSES), F32)
    for iteration in range(ITERS):
        parts = apply_tiles(panel_kernel, CLASSES, source, target, tiles, *gather_panels(panel))
        image, sums = call(
            image_kernel,
            (field, shape((rows, 8, CLASSES))),
            *reduce_parts(parts), label, degree, direction, residual,
        )
        sums = to_everyone(sums, ROW)
        sums = call(relay_kernel, shape((cols, 8, CLASSES)), sums)
        sums = to_everyone(sums, COL)
        state = (sums, norm, solution, residual, direction, image)
        if iteration + 1 < ITERS:
            solution, residual, direction, panel, norm = call(
                functools.partial(step_kernel, iteration == 0),
                (field, field, field, half, shape((1, CLASSES))),
                *state,
            )
        else:
            out = shape((size, CLASSES))
            return call(last_kernel, (out, out), *state)


def solution(mesh):
    torus = Mesh(mesh.devices.reshape(4, 2, 2, 8, 2), AXES)
    return jax.shard_map(
        shards,
        mesh=torus,
        in_specs=(P(AXES, None, None), P(AXES), P(AXES), P(AXES)),
        out_specs=(P(AXES, None), P(AXES, None)),
        check_vma=False,
    )
```

```python
import functools

import jax
import jax.numpy as jnp
from jax import lax
from jax.experimental import pallas as pl
from jax.experimental.pallas import tpu as pltpu
from jax.sharding import Mesh
from jax.sharding import PartitionSpec as P

CLASSES = 128
ITERS = 3
CHAINS = 1
PART = CLASSES // CHAINS
AXES = ("x", "yh", "yl", "z", "core")
ROW = ("x", "yh")
COL = ("yl", "z", "core")
CHIPS = ("yl", "z")
NEAR = ("x", "yh", "yl", "core")
FAR = ("z",)
F32 = jnp.float32
BF16 = jnp.bfloat16
CHUNK = 8
PARAMS = pltpu.CompilerParams(vmem_limit_bytes=50 * 1024 * 1024)
VMEM = pl.BlockSpec(memory_space=pltpu.VMEM)
SMEM = pl.BlockSpec(memory_space=pltpu.SMEM)
HBM = pl.BlockSpec(memory_space=pltpu.HBM)


def shape(dims, dtype=F32):
    return jax.ShapeDtypeStruct(dims, dtype)


def exchange(blocks, axis):
    return lax.all_to_all(blocks, axis, 0, 0, tiled=True)


def call(kernel, out_shape, *args):
    return pl.pallas_call(
        kernel,
        in_specs=[VMEM] * len(args),
        out_specs=jax.tree.map(lambda _: VMEM, out_shape),
        out_shape=out_shape,
        compiler_params=PARAMS,
    )(*args)


def apply_tiles(kernel, out_shape, source, target, tiles, *panels):
    count = tiles.shape[0]
    return pl.pallas_call(
        kernel,
        in_specs=[SMEM, SMEM, HBM] + [VMEM] * len(panels),
        out_specs=jax.tree.map(lambda _: VMEM, out_shape),
        out_shape=out_shape,
        scratch_shapes=[
            pltpu.VMEM(tiles.shape, tiles.dtype),
            pltpu.SemaphoreType.DMA((count // CHUNK,)),
        ],
        compiler_params=PARAMS,
    )(source, target, tiles, *panels)


def each_tile(tiles_ref, held, arrived, work):
    def chunk(step):
        span = pl.ds(step * CHUNK, CHUNK)
        return pltpu.make_async_copy(tiles_ref.at[span], held.at[span], arrived.at[step])

    steps = held.shape[0] // CHUNK
    for step in range(steps):
        chunk(step).start()
    for step in range(steps):
        chunk(step).wait()
        for at in range(step * CHUNK, (step + 1) * CHUNK):
            work(at, held[at])


def label_kernel(source_ref, target_ref, tiles_ref, label_ref, *rest):
    *parts, degree_ref, held, arrived = rest
    size = held.shape[1]
    classes = lax.broadcasted_iota(jnp.int32, (CLASSES, size), 0)
    for part in parts:
        part[...] = jnp.zeros_like(part)
    degree_ref[...] = jnp.zeros_like(degree_ref)

    def work(at, tile):
        hot = jnp.where(label_ref[source_ref[at]] == classes, F32(1.0), F32(0.0))
        panel = jnp.concatenate([hot, jnp.ones((16, size), F32)], axis=0).astype(BF16)
        product = jnp.dot(panel, tile, preferred_element_type=F32)
        target = target_ref[at]
        for h, part in enumerate(parts):
            part[target] += product[h * PART : (h + 1) * PART]
        degree_ref[target] += product[CLASSES : CLASSES + 1]

    each_tile(tiles_ref, held, arrived, work)


def panel_kernel(source_ref, target_ref, tiles_ref, own_ref, other_ref, out_ref, held, arrived):
    half = own_ref.shape[0]
    out_ref[...] = jnp.zeros_like(out_ref)

    def work(at, tile):
        source = source_ref[at]
        place = lax.rem(source, half)
        panel = jnp.where(source < half, own_ref[place], other_ref[place])
        out_ref[target_ref[at]] += jnp.dot(panel, tile, preferred_element_type=F32)

    each_tile(tiles_ref, held, arrived, work)


def diagonal():
    across = lax.broadcasted_iota(jnp.int32, (PART, PART), 1)
    return lax.broadcasted_iota(jnp.int32, (PART, PART), 0) == across


def to_row(column):
    return jnp.sum(jnp.where(diagonal(), column, F32(0.0)), axis=0, keepdims=True)


def to_column(row):
    return jnp.sum(jnp.where(diagonal(), row, F32(0.0)), axis=1, keepdims=True)


def start_kernel(arrived_ref, label_ref, rhs_ref, panels_ref):
    mixed = jnp.sum(arrived_ref[...], axis=0)
    rhs = jnp.where(label_ref[...] < 0, mixed, F32(0.0))
    rhs_ref[...] = rhs
    panel = rhs.astype(BF16)
    for i in range(panels_ref.shape[0]):
        panels_ref[i] = panel


def image_kernel(
    first, arrived_ref, label_ref, degree_ref, direction_ref, residual_ref, image_ref, sums_ref
):
    mixed = jnp.sum(arrived_ref[...], axis=0)
    degree = degree_ref[...]
    direction = direction_ref[...]
    residual = residual_ref[...]
    image = jnp.where(label_ref[...] < 0, degree * direction - mixed, direction)
    image_ref[...] = image
    terms = (direction * image, residual * (residual if first else image), image * image)
    sums = [to_row(jnp.sum(term, axis=1, keepdims=True)) for term in terms]
    sums = jnp.concatenate(sums, axis=1)
    sums_ref[...] = jnp.broadcast_to(sums[None], sums_ref.shape)


def relay_kernel(in_ref, out_ref):
    out_ref[...] = jnp.broadcast_to(jnp.sum(in_ref[...], axis=0)[None], out_ref.shape)


def step_kernel(
    first, sums_ref, norm_ref, solution_ref, residual_ref, direction_ref, image_ref,
    solution_out, residual_out, direction_out, panels_out, norm_out,
):
    sums = jnp.sum(sums_ref[...], axis=0)
    bending, crossed, energy = (sums[:, PART * i : PART * (i + 1)] for i in range(3))
    if first:
        norm, crossed = crossed, bending
    else:
        norm = norm_ref[...]
    alpha = norm / bending
    norm_next = norm - 2.0 * alpha * crossed + alpha * alpha * energy
    norm_out[...] = norm_next
    beta = to_column(norm_next / norm)
    alpha = to_column(alpha)
    direction = direction_ref[...]
    step = alpha * direction
    solution_out[...] = step if first else solution_ref[...] + step
    residual = residual_ref[...] - alpha * image_ref[...]
    residual_out[...] = residual
    direction = residual + beta * direction
    direction_out[...] = direction
    panel = direction.astype(BF16)
    for i in range(panels_out.shape[0]):
        panels_out[i] = panel


def last_kernel(*refs):
    *ins, scores_out, residual_out = refs
    scores, residuals = [], []
    for h in range(CHAINS):
        sums_ref, norm_ref, solution_ref, residual_ref, direction_ref, image_ref = ins[6 * h : 6 * h + 6]
        sums = jnp.sum(sums_ref[...], axis=0)
        alpha = to_column(norm_ref[...] / sums[:, :PART])
        scores.append(8.0 * CLASSES * (solution_ref[...] + alpha * direction_ref[...]))
        residuals.append(residual_ref[...] - alpha * image_ref[...])
    scores_out[...] = jnp.concatenate(scores, axis=0).T
    residual_out[...] = jnp.concatenate(residuals, axis=0).T


def reduce_by_permutes(parts):
    x = lax.axis_index("x")
    parts = parts.reshape(4, 2, *parts.shape[1:])
    total = parts[x]
    for by in range(1, 4):
        moves = [(i, (i + by) % 4) for i in range(4)]
        total = total + lax.ppermute(parts[(x + by) % 4], "x", moves)
    y = lax.axis_index("yh")
    return total[y] + lax.ppermute(total[1 - y], "yh", [(0, 1), (1, 0)])


def shards(tiles, tile_row, tile_col, label_class):
    size = tiles.shape[1]
    near = lax.axis_size(NEAR)
    far = lax.axis_size(FAR)
    rows = lax.axis_size(ROW)
    cols = lax.axis_size(COL)
    chips = lax.axis_size(CHIPS)
    local = tile_row % cols
    mine = local % 2 == lax.axis_index("core")
    source = local // 2 + jnp.where(mine, 0, chips)
    target = tile_col // cols
    label = label_class.reshape(1, size)
    labels = exchange(jnp.broadcast_to(label[None], (cols, 1, size)), COL)
    out_part = shape((rows, PART, size))
    *sent, degree = apply_tiles(
        label_kernel, (*[out_part] * CHAINS, shape((rows, 1, size))), local, target, tiles, labels
    )
    field = shape((PART, size))
    panels_out = shape((chips, PART, size), BF16)
    norm_out = shape((1, PART))
    arrived = [exchange(s, ROW) for s in sent]
    degree = reduce_by_permutes(degree)
    chains = []
    for h in range(CHAINS):
        residual, panels = call(start_kernel, (field, panels_out), arrived[h], label)
        chains.append((residual, residual, residual, panels, jnp.zeros((1, PART), F32)))
    for iteration in range(ITERS):
        states = []
        for solution, residual, direction, panels, norm in chains:
            own = exchange(panels, CHIPS)
            other = lax.ppermute(own, "core", [(0, 1), (1, 0)])
            partial = apply_tiles(panel_kernel, out_part, source, target, tiles, own, other)
            image, sums = call(
                functools.partial(image_kernel, iteration == 0),
                (field, shape((near, 1, 3 * PART))),
                exchange(partial, ROW), label, degree, direction, residual,
            )
            sums = call(relay_kernel, shape((far, 1, 3 * PART)), exchange(sums, NEAR))
            states.append((exchange(sums, FAR), norm, solution, residual, direction, image))
        if iteration + 1 < ITERS:
            step = functools.partial(step_kernel, iteration == 0)
            chains = [call(step, (field, field, field, panels_out, norm_out), *s) for s in states]
    out = shape((size, CLASSES))
    return call(last_kernel, (out, out), *[a for s in states for a in s])


def solution(mesh):
    torus = Mesh(mesh.devices.reshape(4, 2, 2, 8, 2), AXES)
    return jax.shard_map(
        shards,
        mesh=torus,
        in_specs=(P(AXES, None, None), P(AXES), P(AXES), P(AXES)),
        out_specs=(P(AXES, None), P(AXES, None)),
        check_vma=False,
    )
```

```python
import jax
import jax.numpy as jnp
from jax import lax
from jax.experimental import pallas as pl
from jax.experimental.pallas import tpu as pltpu
from jax.sharding import Mesh
from jax.sharding import PartitionSpec as P

CLASSES = 128
SHIFT = 4.0
TINY = 1e-30
AXES = ("x", "yh", "yl", "z", "core")
ROW = ("x", "yh")
COL = ("yl", "z", "core")
CHIPS = ("yl", "z")
NEAR = ("x", "yh", "yl", "core")
FAR = ("z",)
F32 = jnp.float32
BF16 = jnp.bfloat16
CHUNK = 8
PARAMS = pltpu.CompilerParams(vmem_limit_bytes=50 * 1024 * 1024)
VMEM = pl.BlockSpec(memory_space=pltpu.VMEM)
SMEM = pl.BlockSpec(memory_space=pltpu.SMEM)
HBM = pl.BlockSpec(memory_space=pltpu.HBM)


def shape(dims, dtype=F32):
    return jax.ShapeDtypeStruct(dims, dtype)


def exchange(blocks, axis):
    return lax.all_to_all(blocks, axis, 0, 0, tiled=True)


def call(kernel, out_shape, *args):
    return pl.pallas_call(
        kernel,
        in_specs=[VMEM] * len(args),
        out_specs=jax.tree.map(lambda _: VMEM, out_shape),
        out_shape=out_shape,
        compiler_params=PARAMS,
    )(*args)


def apply_tiles(kernel, out_shape, scalars, tiles, *panels):
    count = tiles.shape[0]
    return pl.pallas_call(
        kernel,
        in_specs=[SMEM] * len(scalars) + [HBM] + [VMEM] * len(panels),
        out_specs=jax.tree.map(lambda _: VMEM, out_shape),
        out_shape=out_shape,
        scratch_shapes=[
            pltpu.VMEM(tiles.shape, tiles.dtype),
            pltpu.SemaphoreType.DMA((count // CHUNK,)),
        ],
        compiler_params=PARAMS,
    )(*scalars, tiles, *panels)


def each_tile(tiles_ref, held, arrived, prepare, work):
    def chunk(step):
        span = pl.ds(step * CHUNK, CHUNK)
        return pltpu.make_async_copy(tiles_ref.at[span], held.at[span], arrived.at[step])

    steps = held.shape[0] // CHUNK
    for step in range(steps):
        chunk(step).start()
    prepare()
    for step in range(steps):
        chunk(step).wait()
        for at in range(step * CHUNK, (step + 1) * CHUNK):
            work(at, held[at])


def label_kernel(
    source_ref, target_ref, tiles_ref, label_ref, out_ref, degree_ref, count_ref, held, arrived
):
    size = held.shape[1]
    classes = lax.broadcasted_iota(jnp.int32, (CLASSES, size), 0)

    def prepare():
        out_ref[...] = jnp.zeros_like(out_ref)
        degree_ref[...] = jnp.zeros_like(degree_ref)
        count = jnp.sum(jnp.where(label_ref[...] < 0, F32(1.0), F32(0.0)), axis=0)
        count_ref[...] = jnp.broadcast_to(jnp.sum(count, axis=1, keepdims=True), count_ref.shape)

    def work(at, tile):
        hot = jnp.where(label_ref[source_ref[at]] == classes, F32(1.0), F32(0.0))
        panel = jnp.concatenate([hot, jnp.ones((16, size), F32)], axis=0).astype(BF16)
        product = jnp.dot(panel, tile, preferred_element_type=F32)
        target = target_ref[at]
        out_ref[target] += product[:CLASSES]
        degree_ref[target] += product[CLASSES : CLASSES + 1]

    each_tile(tiles_ref, held, arrived, prepare, work)


def total_of(panels_ref):
    total = panels_ref[0].astype(F32)
    for i in range(1, panels_ref.shape[0]):
        total = total + panels_ref[i].astype(F32)
    return jnp.sum(jnp.sum(total, axis=0, keepdims=True), axis=1, keepdims=True)


def multiply_panels(source_ref, target_ref, tiles_ref, own_ref, other_ref, out_ref, held, arrived, prepare):
    half = own_ref.shape[0]

    def work(at, tile):
        source = source_ref[at]
        place = lax.rem(source, half)
        panel = jnp.where(source < half, own_ref[place], other_ref[place])
        out_ref[target_ref[at]] += jnp.dot(panel, tile, preferred_element_type=F32)

    each_tile(tiles_ref, held, arrived, prepare, work)


def first_panel_kernel(
    source_ref, target_ref, tiles_ref, own_ref, other_ref, count_ref, out_ref, shift_ref, held, arrived
):
    def prepare():
        out_ref[...] = jnp.zeros_like(out_ref)
        total = total_of(own_ref) + total_of(other_ref)
        shift_ref[...] = SHIFT * total / jnp.maximum(count_ref[...], 1.0)

    multiply_panels(
        source_ref, target_ref, tiles_ref, own_ref, other_ref, out_ref, held, arrived, prepare
    )


def shifted_panel_kernel(
    source_ref, target_ref, tiles_ref, own_ref, other_ref, last_ref, shift_ref, out_ref, held, arrived
):
    def prepare():
        for i in range(out_ref.shape[0]):
            out_ref[i] = shift_ref[:, :1] * last_ref[i]

    multiply_panels(
        source_ref, target_ref, tiles_ref, own_ref, other_ref, out_ref, held, arrived, prepare
    )


def panel_kernel(source_ref, target_ref, tiles_ref, own_ref, other_ref, out_ref, held, arrived):
    def prepare():
        out_ref[...] = jnp.zeros_like(out_ref)

    multiply_panels(
        source_ref, target_ref, tiles_ref, own_ref, other_ref, out_ref, held, arrived, prepare
    )


def diagonal():
    across = lax.broadcasted_iota(jnp.int32, (CLASSES, CLASSES), 1)
    return lax.broadcasted_iota(jnp.int32, (CLASSES, CLASSES), 0) == across


def to_row(column):
    return jnp.sum(jnp.where(diagonal(), column, F32(0.0)), axis=0, keepdims=True)


def to_column(row):
    return jnp.sum(jnp.where(diagonal(), row, F32(0.0)), axis=1, keepdims=True)


def to_all(value, copies_ref):
    for i in range(copies_ref.shape[0]):
        copies_ref[i] = value


def start_kernel(arrived_ref, label_ref, rhs_ref, panels_ref):
    mixed = jnp.sum(arrived_ref[...], axis=0)
    rhs = jnp.where(label_ref[...] < 0, mixed, F32(0.0))
    rhs_ref[...] = rhs
    to_all(rhs.astype(BF16), panels_ref)


def applied(arrived_ref, label_ref, degree_ref, field):
    mixed = jnp.sum(arrived_ref[...], axis=0)
    return jnp.where(label_ref[...] < 0, degree_ref[...] * field - mixed, field)


def inner_products(pairs, sums_ref, more=()):
    sums = [to_row(jnp.sum(a * b, axis=1, keepdims=True)) for a, b in pairs]
    to_all(jnp.concatenate([*sums, *more], axis=1), sums_ref)


def image_kernel(arrived_ref, label_ref, degree_ref, shift_ref, rhs_ref, image_ref, panels_ref):
    rhs = rhs_ref[...]
    image = applied(arrived_ref, label_ref, degree_ref, rhs)
    image_ref[...] = image
    to_all((image - shift_ref[:, :1] * rhs).astype(BF16), panels_ref)


TIMES = (0, 1, 2, 2, 3, 4)


def second_kernel(arrived_ref, label_ref, degree_ref, rhs_ref, image_ref, second_ref, sums_ref):
    rhs, image = rhs_ref[...], image_ref[...]
    second = applied(arrived_ref, label_ref, degree_ref, image)
    second_ref[...] = second
    degree = degree_ref[...]
    scale = jnp.sum(degree, axis=1, keepdims=True) / degree.shape[1]
    scale = jnp.maximum(scale, F32(TINY))
    image = image / scale
    second = second / scale / scale
    pairs = ((rhs, rhs), (rhs, image), (image, image), (rhs, second), (image, second), (second, second))
    inner_products(pairs, sums_ref, [jnp.broadcast_to(scale, (1, CLASSES))])


def pooled(sums):
    part = [sums[:, :, CLASSES * i : CLASSES * (i + 1)] for i in range(7)]
    scale = jnp.max(part[6], axis=0)
    powers = [jnp.ones_like(part[6]), part[6] / scale[None]]
    for _ in range(3):
        powers.append(powers[-1] * powers[1])
    return [jnp.sum(p * powers[t], axis=0) for p, t in zip(part, TIMES)] + [scale]


def pool_kernel(in_ref, out_ref):
    to_all(jnp.concatenate(pooled(in_ref[...]), axis=1), out_ref)


def relay_kernel(in_ref, out_ref):
    to_all(jnp.sum(in_ref[...], axis=0), out_ref)


def two_steps_kernel(
    sums_ref, rhs_ref, image_ref, second_ref,
    solution_out, residual_out, direction_out, panels_out, norm_out,
):
    bb, bp, pp, bs, ps, ss, scale = pooled(sums_ref[...])
    alpha = bb / bp
    norm = bb - 2.0 * alpha * bp + alpha * alpha * pp
    beta = norm / bb
    more = 1.0 + beta
    square = alpha * alpha
    bending = more * more * bp - alpha * more * (bs + pp) + square * ps
    crossed = more * bp - alpha * bs - alpha * more * pp + square * ps
    energy = more * more * pp - 2.0 * alpha * more * ps + square * ss
    alpha_next = norm / bending
    norm_next = norm - 2.0 * alpha_next * crossed + alpha_next * alpha_next * energy
    norm_out[...] = norm_next
    beta_next = to_column(norm_next / norm)
    alpha, alpha_next = to_column(alpha / scale), to_column(alpha_next / scale)
    beta = to_column(beta)
    rhs, image = rhs_ref[...], image_ref[...]
    residual = rhs - alpha * image
    direction = residual + beta * rhs
    solution_out[...] = alpha * rhs + alpha_next * direction
    image_next = (1.0 + beta) * image - alpha * second_ref[...]
    residual = residual - alpha_next * image_next
    residual_out[...] = residual
    direction = residual + beta_next * direction
    direction_out[...] = direction
    to_all(direction.astype(BF16), panels_out)


def third_kernel(arrived_ref, label_ref, degree_ref, direction_ref, image_ref, sums_ref):
    direction = direction_ref[...]
    image = applied(arrived_ref, label_ref, degree_ref, direction)
    image_ref[...] = image
    inner_products(((direction, image),), sums_ref)


def last_kernel(
    sums_ref, norm_ref, solution_ref, residual_ref, direction_ref, image_ref,
    scores_out, residual_out,
):
    alpha = to_column(norm_ref[...] / jnp.sum(sums_ref[...], axis=0))
    total = solution_ref[...] + alpha * direction_ref[...]
    scores_out[...] = (8.0 * CLASSES * total).T
    residual_out[...] = (residual_ref[...] - alpha * image_ref[...]).T


def reduce_by_permutes(parts):
    x = lax.axis_index("x")
    parts = parts.reshape(4, 2, *parts.shape[1:])
    total = parts[x]
    for by in range(1, 4):
        moves = [(i, (i + by) % 4) for i in range(4)]
        total = total + lax.ppermute(parts[(x + by) % 4], "x", moves)
    y = lax.axis_index("yh")
    return total[y] + lax.ppermute(total[1 - y], "yh", [(0, 1), (1, 0)])


def shards(tiles, tile_row, tile_col, label_class):
    size = tiles.shape[1]
    near = lax.axis_size(NEAR)
    far = lax.axis_size(FAR)
    rows = lax.axis_size(ROW)
    cols = lax.axis_size(COL)
    chips = lax.axis_size(CHIPS)
    local = tile_row % cols
    mine = local % 2 == lax.axis_index("core")
    source = local // 2 + jnp.where(mine, 0, chips)
    target = tile_col // cols
    label = label_class.reshape(1, size)
    partial_out = shape((rows, CLASSES, size))
    field = shape((CLASSES, size))
    panels_out = shape((chips, CLASSES, size), BF16)
    row_out = shape((1, CLASSES))

    def gather(panels):
        own = exchange(panels, CHIPS)
        return own, lax.ppermute(own, "core", [(0, 1), (1, 0)])

    def everywhere(kernel, sums):
        sums = exchange(sums, NEAR)
        return exchange(call(kernel, shape((far, *sums.shape[1:])), sums), FAR)

    labels = exchange(jnp.broadcast_to(label[None], (cols, 1, size)), COL)
    partial, share, count = apply_tiles(
        label_kernel, (partial_out, shape((rows, 1, size)), row_out), (local, target), tiles, labels
    )
    rhs, panels = call(start_kernel, (field, panels_out), exchange(partial, ROW), label)
    degree = reduce_by_permutes(share)
    partial, shift = apply_tiles(
        first_panel_kernel, (partial_out, row_out), (source, target), tiles, *gather(panels), count
    )
    image, panels = call(
        image_kernel, (field, panels_out), exchange(partial, ROW), label, degree, shift, rhs
    )
    partial = apply_tiles(
        shifted_panel_kernel, partial_out, (source, target), tiles, *gather(panels), partial, shift
    )
    second, sums = call(
        second_kernel, (field, shape((near, 1, 7 * CLASSES))),
        exchange(partial, ROW), label, degree, rhs, image,
    )
    solution, residual, direction, panels, norm = call(
        two_steps_kernel, (field, field, field, panels_out, row_out),
        everywhere(pool_kernel, sums), rhs, image, second,
    )
    partial = apply_tiles(panel_kernel, partial_out, (source, target), tiles, *gather(panels))
    image, sums = call(
        third_kernel, (field, shape((near, 1, CLASSES))),
        exchange(partial, ROW), label, degree, direction,
    )
    out = shape((size, CLASSES))
    return call(
        last_kernel, (out, out), everywhere(relay_kernel, sums), norm, solution, residual, direction, image
    )


def solution(mesh):
    torus = Mesh(mesh.devices.reshape(4, 2, 2, 8, 2), AXES)
    return jax.shard_map(
        shards,
        mesh=torus,
        in_specs=(P(AXES, None, None), P(AXES), P(AXES), P(AXES)),
        out_specs=(P(AXES, None), P(AXES, None)),
        check_vma=False,
    )
```

```python
import jax
import jax.numpy as jnp
from jax import lax
from jax.experimental import pallas as pl
from jax.experimental.pallas import tpu as pltpu
from jax.sharding import Mesh
from jax.sharding import PartitionSpec as P

CLASSES = 128
SHIFT = 4.0
TINY = 1e-30
AXES = ("x", "yh", "yl", "z", "core")
ROW = ("x", "yh")
COL = ("yl", "z", "core")
CHIPS = ("yl", "z")
NEAR = ("x", "yh", "yl", "core")
FAR = ("z",)
F32 = jnp.float32
BF16 = jnp.bfloat16
CHUNK = 16
PARAMS = pltpu.CompilerParams(vmem_limit_bytes=50 * 1024 * 1024)
VMEM = pl.BlockSpec(memory_space=pltpu.VMEM)
SMEM = pl.BlockSpec(memory_space=pltpu.SMEM)
HBM = pl.BlockSpec(memory_space=pltpu.HBM)


def shape(dims, dtype=F32):
    return jax.ShapeDtypeStruct(dims, dtype)


def exchange(blocks, axis):
    return lax.all_to_all(blocks, axis, 0, 0, tiled=True)


def call(kernel, out_shape, *args):
    return pl.pallas_call(
        kernel,
        in_specs=[VMEM] * len(args),
        out_specs=jax.tree.map(lambda _: VMEM, out_shape),
        out_shape=out_shape,
        compiler_params=PARAMS,
    )(*args)


def apply_tiles(kernel, out_shape, scalars, tiles, *panels):
    count = tiles.shape[0]
    return pl.pallas_call(
        kernel,
        in_specs=[SMEM] * len(scalars) + [HBM] + [VMEM] * len(panels),
        out_specs=jax.tree.map(lambda _: VMEM, out_shape),
        out_shape=out_shape,
        scratch_shapes=[
            pltpu.VMEM(tiles.shape, tiles.dtype),
            pltpu.SemaphoreType.DMA((count // CHUNK,)),
        ],
        compiler_params=PARAMS,
    )(*scalars, tiles, *panels)


def each_tile(tiles_ref, held, arrived, prepare, work):
    def chunk(step):
        span = pl.ds(step * CHUNK, CHUNK)
        return pltpu.make_async_copy(tiles_ref.at[span], held.at[span], arrived.at[step])

    steps = held.shape[0] // CHUNK
    for step in range(steps):
        chunk(step).start()
    prepare()
    for step in range(steps):
        chunk(step).wait()
        for at in range(step * CHUNK, (step + 1) * CHUNK):
            work(at, held[at])


def label_kernel(
    source_ref, target_ref, tiles_ref, label_ref, out_ref, degree_ref, count_ref, held, arrived
):
    size = held.shape[1]
    classes = lax.broadcasted_iota(jnp.int32, (CLASSES, size), 0)

    def prepare():
        out_ref[...] = jnp.zeros_like(out_ref)
        degree_ref[...] = jnp.zeros_like(degree_ref)
        count = jnp.sum(jnp.where(label_ref[...] < 0, F32(1.0), F32(0.0)), axis=0)
        count_ref[...] = jnp.broadcast_to(jnp.sum(count, axis=1, keepdims=True), count_ref.shape)

    def work(at, tile):
        hot = jnp.where(label_ref[source_ref[at]] == classes, F32(1.0), F32(0.0))
        panel = jnp.concatenate([hot, jnp.ones((16, size), F32)], axis=0).astype(BF16)
        product = jnp.dot(panel, tile, preferred_element_type=F32)
        target = target_ref[at]
        out_ref[target] += product[:CLASSES]
        degree_ref[target] += product[CLASSES : CLASSES + 1]

    each_tile(tiles_ref, held, arrived, prepare, work)


def total_of(panels_ref):
    total = panels_ref[0].astype(F32)
    for i in range(1, panels_ref.shape[0]):
        total = total + panels_ref[i].astype(F32)
    return jnp.sum(jnp.sum(total, axis=0, keepdims=True), axis=1, keepdims=True)


def multiply_panels(source_ref, target_ref, tiles_ref, own_ref, other_ref, out_ref, held, arrived, prepare):
    half = own_ref.shape[0]

    def work(at, tile):
        source = source_ref[at]
        place = lax.rem(source, half)
        panel = jnp.where(source < half, own_ref[place], other_ref[place])
        out_ref[target_ref[at]] += jnp.dot(panel, tile, preferred_element_type=F32)

    each_tile(tiles_ref, held, arrived, prepare, work)


def first_panel_kernel(
    source_ref, target_ref, tiles_ref, own_ref, other_ref, count_ref, out_ref, shift_ref, held, arrived
):
    def prepare():
        out_ref[...] = jnp.zeros_like(out_ref)
        total = total_of(own_ref) + total_of(other_ref)
        shift_ref[...] = SHIFT * total / jnp.maximum(count_ref[...], 1.0)

    multiply_panels(
        source_ref, target_ref, tiles_ref, own_ref, other_ref, out_ref, held, arrived, prepare
    )


def shifted_panel_kernel(
    source_ref, target_ref, tiles_ref, own_ref, other_ref, last_ref, shift_ref, out_ref, held, arrived
):
    def prepare():
        for i in range(out_ref.shape[0]):
            out_ref[i] = shift_ref[:, :1] * last_ref[i]

    multiply_panels(
        source_ref, target_ref, tiles_ref, own_ref, other_ref, out_ref, held, arrived, prepare
    )


def panel_kernel(source_ref, target_ref, tiles_ref, own_ref, other_ref, out_ref, held, arrived):
    def prepare():
        out_ref[...] = jnp.zeros_like(out_ref)

    multiply_panels(
        source_ref, target_ref, tiles_ref, own_ref, other_ref, out_ref, held, arrived, prepare
    )


def diagonal():
    across = lax.broadcasted_iota(jnp.int32, (CLASSES, CLASSES), 1)
    return lax.broadcasted_iota(jnp.int32, (CLASSES, CLASSES), 0) == across


def to_row(column):
    return jnp.sum(jnp.where(diagonal(), column, F32(0.0)), axis=0, keepdims=True)


def to_column(row):
    return jnp.sum(jnp.where(diagonal(), row, F32(0.0)), axis=1, keepdims=True)


def to_all(value, copies_ref):
    for i in range(copies_ref.shape[0]):
        copies_ref[i] = value


def start_kernel(arrived_ref, label_ref, rhs_ref, panels_ref):
    mixed = jnp.sum(arrived_ref[...], axis=0)
    rhs = jnp.where(label_ref[...] < 0, mixed, F32(0.0))
    rhs_ref[...] = rhs
    to_all(rhs.astype(BF16), panels_ref)


def applied(arrived_ref, label_ref, degree_ref, field):
    mixed = jnp.sum(arrived_ref[...], axis=0)
    return jnp.where(label_ref[...] < 0, degree_ref[...] * field - mixed, field)


def inner_products(pairs, sums_ref, more=()):
    sums = [to_row(jnp.sum(a * b, axis=1, keepdims=True)) for a, b in pairs]
    to_all(jnp.concatenate([*sums, *more], axis=1), sums_ref)


def image_kernel(arrived_ref, label_ref, degree_ref, shift_ref, rhs_ref, image_ref, panels_ref):
    rhs = rhs_ref[...]
    image = applied(arrived_ref, label_ref, degree_ref, rhs)
    image_ref[...] = image
    to_all((image - shift_ref[:, :1] * rhs).astype(BF16), panels_ref)


TIMES = (0, 1, 2, 2, 3, 4)


def second_kernel(arrived_ref, label_ref, degree_ref, rhs_ref, image_ref, second_ref, sums_ref):
    rhs, image = rhs_ref[...], image_ref[...]
    second = applied(arrived_ref, label_ref, degree_ref, image)
    second_ref[...] = second
    degree = degree_ref[...]
    scale = jnp.sum(degree, axis=1, keepdims=True) / degree.shape[1]
    scale = jnp.maximum(scale, F32(TINY))
    image = image / scale
    second = second / scale / scale
    pairs = ((rhs, rhs), (rhs, image), (image, image), (rhs, second), (image, second), (second, second))
    inner_products(pairs, sums_ref, [jnp.broadcast_to(scale, (1, CLASSES))])


def pooled(sums):
    part = [sums[:, :, CLASSES * i : CLASSES * (i + 1)] for i in range(7)]
    scale = jnp.max(part[6], axis=0)
    powers = [jnp.ones_like(part[6]), part[6] / scale[None]]
    for _ in range(3):
        powers.append(powers[-1] * powers[1])
    return [jnp.sum(p * powers[t], axis=0) for p, t in zip(part, TIMES)] + [scale]


def pool_kernel(in_ref, out_ref):
    to_all(jnp.concatenate(pooled(in_ref[...]), axis=1), out_ref)


def two_steps_kernel(
    sums_ref, rhs_ref, image_ref, second_ref,
    solution_out, residual_out, direction_out, panels_out, norm_out,
):
    bb, bp, pp, bs, ps, ss, scale = pooled(sums_ref[...])
    alpha = bb / bp
    norm = bb - 2.0 * alpha * bp + alpha * alpha * pp
    beta = norm / bb
    more = 1.0 + beta
    square = alpha * alpha
    bending = more * more * bp - alpha * more * (bs + pp) + square * ps
    crossed = more * bp - alpha * bs - alpha * more * pp + square * ps
    energy = more * more * pp - 2.0 * alpha * more * ps + square * ss
    alpha_next = norm / bending
    norm_next = norm - 2.0 * alpha_next * crossed + alpha_next * alpha_next * energy
    norm_out[...] = norm_next
    beta_next = to_column(norm_next / norm)
    alpha, alpha_next = to_column(alpha / scale), to_column(alpha_next / scale)
    beta = to_column(beta)
    rhs, image = rhs_ref[...], image_ref[...]
    residual = rhs - alpha * image
    direction = residual + beta * rhs
    solution_out[...] = alpha * rhs + alpha_next * direction
    image_next = (1.0 + beta) * image - alpha * second_ref[...]
    residual = residual - alpha_next * image_next
    residual_out[...] = residual
    direction = residual + beta_next * direction
    direction_out[...] = direction
    to_all(direction.astype(BF16), panels_out)


def third_kernel(arrived_ref, label_ref, degree_ref, direction_ref, image_ref, sums_ref):
    direction = direction_ref[...]
    image = applied(arrived_ref, label_ref, degree_ref, direction)
    image_ref[...] = image
    inner_products(((direction, image),), sums_ref)


def last_kernel(
    sums_ref, norm_ref, solution_ref, residual_ref, direction_ref, image_ref,
    scores_out, residual_out,
):
    alpha = to_column(norm_ref[...] / jnp.sum(sums_ref[...], axis=0))
    total = solution_ref[...] + alpha * direction_ref[...]
    scores_out[...] = (8.0 * CLASSES * total).T
    residual_out[...] = (residual_ref[...] - alpha * image_ref[...]).T


def after_kernel(own_ref, degree_ref, own_out, degree_out):
    degree_out[...] = degree_ref[...]


def after(own, degree):
    return pl.pallas_call(
        after_kernel,
        in_specs=[pl.BlockSpec(memory_space=pl.ANY), VMEM],
        out_specs=[pl.BlockSpec(memory_space=pl.ANY), VMEM],
        out_shape=[shape(own.shape, own.dtype), shape(degree.shape)],
        input_output_aliases={0: 0},
        compiler_params=PARAMS,
    )(own, degree)


def reduce_by_permutes(parts):
    x = lax.axis_index("x")
    parts = parts.reshape(4, 2, *parts.shape[1:])
    total = parts[x]
    for by in range(1, 4):
        moves = [(i, (i + by) % 4) for i in range(4)]
        total = total + lax.ppermute(parts[(x + by) % 4], "x", moves)
    y = lax.axis_index("yh")
    return total[y] + lax.ppermute(total[1 - y], "yh", [(0, 1), (1, 0)])


def shards(tiles, tile_row, tile_col, label_class):
    size = tiles.shape[1]
    near = lax.axis_size(NEAR)
    far = lax.axis_size(FAR)
    rows = lax.axis_size(ROW)
    cols = lax.axis_size(COL)
    chips = lax.axis_size(CHIPS)
    local = tile_row % cols
    mine = local % 2 == lax.axis_index("core")
    source = local // 2 + jnp.where(mine, 0, chips)
    target = tile_col // cols
    label = label_class.reshape(1, size)
    partial_out = shape((rows, CLASSES, size))
    field = shape((CLASSES, size))
    panels_out = shape((chips, CLASSES, size), BF16)
    row_out = shape((1, CLASSES))

    def other_core(own):
        return lax.ppermute(own, "core", [(0, 1), (1, 0)])

    def gather(panels):
        own = exchange(panels, CHIPS)
        return own, other_core(own)

    def everywhere(sums):
        sums = exchange(sums, NEAR)
        return exchange(call(pool_kernel, shape((far, *sums.shape[1:])), sums), FAR)

    labels = exchange(jnp.broadcast_to(label[None], (cols, 1, size)), COL)
    partial, share, count = apply_tiles(
        label_kernel, (partial_out, shape((rows, 1, size)), row_out), (local, target), tiles, labels
    )
    rhs, panels = call(start_kernel, (field, panels_out), exchange(partial, ROW), label)
    own, degree = after(exchange(panels, CHIPS), reduce_by_permutes(share))
    partial, shift = apply_tiles(
        first_panel_kernel, (partial_out, row_out), (source, target), tiles, own, other_core(own), count
    )
    image, panels = call(
        image_kernel, (field, panels_out), exchange(partial, ROW), label, degree, shift, rhs
    )
    partial = apply_tiles(
        shifted_panel_kernel, partial_out, (source, target), tiles, *gather(panels), partial, shift
    )
    second, sums = call(
        second_kernel, (field, shape((near, 1, 7 * CLASSES))),
        exchange(partial, ROW), label, degree, rhs, image,
    )
    solution, residual, direction, panels, norm = call(
        two_steps_kernel, (field, field, field, panels_out, row_out),
        everywhere(sums), rhs, image, second,
    )
    partial = apply_tiles(panel_kernel, partial_out, (source, target), tiles, *gather(panels))
    image, sums = call(
        third_kernel, (field, shape((near * far, 1, CLASSES))),
        exchange(partial, ROW), label, degree, direction,
    )
    out = shape((size, CLASSES))
    return call(
        last_kernel, (out, out), exchange(sums, AXES), norm, solution, residual, direction, image
    )


def solution(mesh):
    torus = Mesh(mesh.devices.reshape(4, 2, 2, 8, 2), AXES)
    return jax.shard_map(
        shards,
        mesh=torus,
        in_specs=(P(AXES, None, None), P(AXES), P(AXES), P(AXES)),
        out_specs=(P(AXES, None), P(AXES, None)),
        check_vma=False,
    )
```

```python
import jax
import jax.numpy as jnp
from jax import lax
from jax.experimental import pallas as pl
from jax.experimental.pallas import tpu as pltpu
from jax.sharding import Mesh
from jax.sharding import PartitionSpec as P

CLASSES = 128
SHIFT = 4.0
TINY = 1e-30
AXES = ("x", "yh", "yl", "z", "core")
ROW = ("x", "yh")
COL = ("yl", "z", "core")
CHIPS = ("yl", "z")
NEAR = ("x", "yh", "yl")
FAR = ("z", "core")
F32 = jnp.float32
BF16 = jnp.bfloat16
CHUNK = 16
PARAMS = pltpu.CompilerParams(vmem_limit_bytes=50 * 1024 * 1024)
VMEM = pl.BlockSpec(memory_space=pltpu.VMEM)
SMEM = pl.BlockSpec(memory_space=pltpu.SMEM)
HBM = pl.BlockSpec(memory_space=pltpu.HBM)


def shape(dims, dtype=F32):
    return jax.ShapeDtypeStruct(dims, dtype)


def exchange(blocks, axis):
    return lax.all_to_all(blocks, axis, 0, 0, tiled=True)


def call(kernel, out_shape, *args):
    return pl.pallas_call(
        kernel,
        in_specs=[VMEM] * len(args),
        out_specs=jax.tree.map(lambda _: VMEM, out_shape),
        out_shape=out_shape,
        compiler_params=PARAMS,
    )(*args)


def apply_tiles(kernel, out_shape, scalars, tiles, *panels):
    count = tiles.shape[0]
    return pl.pallas_call(
        kernel,
        in_specs=[SMEM] * len(scalars) + [HBM] + [VMEM] * len(panels),
        out_specs=jax.tree.map(lambda _: VMEM, out_shape),
        out_shape=out_shape,
        scratch_shapes=[
            pltpu.VMEM(tiles.shape, tiles.dtype),
            pltpu.SemaphoreType.DMA((count // CHUNK,)),
        ],
        compiler_params=PARAMS,
    )(*scalars, tiles, *panels)


def each_tile(tiles_ref, held, arrived, prepare, work):
    def chunk(step):
        span = pl.ds(step * CHUNK, CHUNK)
        return pltpu.make_async_copy(tiles_ref.at[span], held.at[span], arrived.at[step])

    steps = held.shape[0] // CHUNK
    for step in range(steps):
        chunk(step).start()
    prepare()
    for step in range(steps):
        chunk(step).wait()
        for at in range(step * CHUNK, (step + 1) * CHUNK):
            work(at, held[at])


def label_kernel(
    source_ref, target_ref, tiles_ref, label_ref, out_ref, degree_ref, count_ref, held, arrived
):
    size = held.shape[1]
    classes = lax.broadcasted_iota(jnp.int32, (CLASSES, size), 0)

    def prepare():
        out_ref[...] = jnp.zeros_like(out_ref)
        degree_ref[...] = jnp.zeros_like(degree_ref)
        count = jnp.sum(jnp.where(label_ref[...] < 0, F32(1.0), F32(0.0)), axis=0)
        count_ref[...] = jnp.broadcast_to(jnp.sum(count, axis=1, keepdims=True), count_ref.shape)

    def work(at, tile):
        hot = jnp.where(label_ref[source_ref[at]] == classes, F32(1.0), F32(0.0))
        panel = jnp.concatenate([hot, jnp.ones((16, size), F32)], axis=0).astype(BF16)
        product = jnp.dot(panel, tile, preferred_element_type=F32)
        target = target_ref[at]
        out_ref[target] += product[:CLASSES]
        degree_ref[target] += product[CLASSES : CLASSES + 1]

    each_tile(tiles_ref, held, arrived, prepare, work)


def total_of(panels_ref):
    total = panels_ref[0].astype(F32)
    for i in range(1, panels_ref.shape[0]):
        total = total + panels_ref[i].astype(F32)
    return jnp.sum(jnp.sum(total, axis=0, keepdims=True), axis=1, keepdims=True)


def multiply_panels(source_ref, target_ref, tiles_ref, own_ref, other_ref, out_ref, held, arrived, prepare):
    half = own_ref.shape[0]

    def work(at, tile):
        source = source_ref[at]
        place = lax.rem(source, half)
        panel = jnp.where(source < half, own_ref[place], other_ref[place])
        out_ref[target_ref[at]] += jnp.dot(panel, tile, preferred_element_type=F32)

    each_tile(tiles_ref, held, arrived, prepare, work)


def first_panel_kernel(
    source_ref, target_ref, tiles_ref, own_ref, other_ref, count_ref, out_ref, shift_ref, held, arrived
):
    def prepare():
        out_ref[...] = jnp.zeros_like(out_ref)
        total = total_of(own_ref) + total_of(other_ref)
        shift_ref[...] = SHIFT * total / jnp.maximum(count_ref[...], 1.0)

    multiply_panels(
        source_ref, target_ref, tiles_ref, own_ref, other_ref, out_ref, held, arrived, prepare
    )


def shifted_panel_kernel(
    source_ref, target_ref, tiles_ref, own_ref, other_ref, last_ref, shift_ref, out_ref, held, arrived
):
    def prepare():
        for i in range(out_ref.shape[0]):
            out_ref[i] = shift_ref[:, :1] * last_ref[i]

    multiply_panels(
        source_ref, target_ref, tiles_ref, own_ref, other_ref, out_ref, held, arrived, prepare
    )


def panel_kernel(source_ref, target_ref, tiles_ref, own_ref, other_ref, out_ref, held, arrived):
    def prepare():
        out_ref[...] = jnp.zeros_like(out_ref)

    multiply_panels(
        source_ref, target_ref, tiles_ref, own_ref, other_ref, out_ref, held, arrived, prepare
    )


def diagonal():
    across = lax.broadcasted_iota(jnp.int32, (CLASSES, CLASSES), 1)
    return lax.broadcasted_iota(jnp.int32, (CLASSES, CLASSES), 0) == across


def to_row(column):
    return jnp.sum(jnp.where(diagonal(), column, F32(0.0)), axis=0, keepdims=True)


def to_column(row):
    return jnp.sum(jnp.where(diagonal(), row, F32(0.0)), axis=1, keepdims=True)


def to_all(value, copies_ref):
    for i in range(copies_ref.shape[0]):
        copies_ref[i] = value


def start_kernel(arrived_ref, label_ref, rhs_ref, panels_ref):
    mixed = jnp.sum(arrived_ref[...], axis=0)
    rhs = jnp.where(label_ref[...] < 0, mixed, F32(0.0))
    rhs_ref[...] = rhs
    to_all(rhs.astype(BF16), panels_ref)


def applied(arrived_ref, label_ref, degree_ref, field):
    mixed = jnp.sum(arrived_ref[...], axis=0)
    return jnp.where(label_ref[...] < 0, degree_ref[...] * field - mixed, field)


def inner_products(pairs, sums_ref, more=()):
    sums = [to_row(jnp.sum(a * b, axis=1, keepdims=True)) for a, b in pairs]
    to_all(jnp.concatenate([*sums, *more], axis=1), sums_ref)


def image_kernel(arrived_ref, label_ref, degree_ref, shift_ref, rhs_ref, image_ref, panels_ref):
    rhs = rhs_ref[...]
    image = applied(arrived_ref, label_ref, degree_ref, rhs)
    image_ref[...] = image
    to_all((image - shift_ref[:, :1] * rhs).astype(BF16), panels_ref)


TIMES = (0, 1, 2, 2, 3, 4)


def second_kernel(arrived_ref, label_ref, degree_ref, rhs_ref, image_ref, second_ref, sums_ref):
    rhs, image = rhs_ref[...], image_ref[...]
    second = applied(arrived_ref, label_ref, degree_ref, image)
    second_ref[...] = second
    degree = degree_ref[...]
    scale = jnp.sum(degree, axis=1, keepdims=True) / degree.shape[1]
    scale = jnp.maximum(scale, F32(TINY))
    image = image / scale
    second = second / scale / scale
    pairs = ((rhs, rhs), (rhs, image), (image, image), (rhs, second), (image, second), (second, second))
    inner_products(pairs, sums_ref, [jnp.broadcast_to(scale, (1, CLASSES))])


def pooled(sums):
    part = [sums[:, :, CLASSES * i : CLASSES * (i + 1)] for i in range(7)]
    scale = jnp.max(part[6], axis=0)
    powers = [jnp.ones_like(part[6]), part[6] / scale[None]]
    for _ in range(3):
        powers.append(powers[-1] * powers[1])
    return [jnp.sum(p * powers[t], axis=0) for p, t in zip(part, TIMES)] + [scale]


def pool_kernel(in_ref, out_ref):
    to_all(jnp.concatenate(pooled(in_ref[...]), axis=1), out_ref)


def two_steps_kernel(
    sums_ref, rhs_ref, image_ref, second_ref,
    solution_out, residual_out, direction_out, panels_out, norm_out,
):
    bb, bp, pp, bs, ps, ss, scale = pooled(sums_ref[...])
    alpha = bb / bp
    norm = bb - 2.0 * alpha * bp + alpha * alpha * pp
    beta = norm / bb
    more = 1.0 + beta
    square = alpha * alpha
    bending = more * more * bp - alpha * more * (bs + pp) + square * ps
    crossed = more * bp - alpha * bs - alpha * more * pp + square * ps
    energy = more * more * pp - 2.0 * alpha * more * ps + square * ss
    alpha_next = norm / bending
    norm_next = norm - 2.0 * alpha_next * crossed + alpha_next * alpha_next * energy
    norm_out[...] = norm_next
    beta_next = to_column(norm_next / norm)
    alpha, alpha_next = to_column(alpha / scale), to_column(alpha_next / scale)
    beta = to_column(beta)
    rhs, image = rhs_ref[...], image_ref[...]
    residual = rhs - alpha * image
    direction = residual + beta * rhs
    solution_out[...] = alpha * rhs + alpha_next * direction
    image_next = (1.0 + beta) * image - alpha * second_ref[...]
    residual = residual - alpha_next * image_next
    residual_out[...] = residual
    direction = residual + beta_next * direction
    direction_out[...] = direction
    to_all(direction.astype(BF16), panels_out)


def third_kernel(arrived_ref, label_ref, degree_ref, direction_ref, image_ref, sums_ref):
    direction = direction_ref[...]
    image = applied(arrived_ref, label_ref, degree_ref, direction)
    image_ref[...] = image
    inner_products(((direction, image),), sums_ref)


def last_kernel(
    sums_ref, norm_ref, solution_ref, residual_ref, direction_ref, image_ref,
    scores_out, residual_out,
):
    alpha = to_column(norm_ref[...] / jnp.sum(sums_ref[...], axis=0))
    total = solution_ref[...] + alpha * direction_ref[...]
    scores_out[...] = (8.0 * CLASSES * total).T
    residual_out[...] = (residual_ref[...] - alpha * image_ref[...]).T


def after_kernel(own_ref, degree_ref, own_out, degree_out):
    degree_out[...] = degree_ref[...]


def after(own, degree):
    return pl.pallas_call(
        after_kernel,
        in_specs=[pl.BlockSpec(memory_space=pl.ANY), VMEM],
        out_specs=[pl.BlockSpec(memory_space=pl.ANY), VMEM],
        out_shape=[shape(own.shape, own.dtype), shape(degree.shape)],
        input_output_aliases={0: 0},
        compiler_params=PARAMS,
    )(own, degree)


def reduce_by_permutes(parts):
    x = lax.axis_index("x")
    parts = parts.reshape(4, 2, *parts.shape[1:])
    total = parts[x]
    for by in range(1, 4):
        moves = [(i, (i + by) % 4) for i in range(4)]
        total = total + lax.ppermute(parts[(x + by) % 4], "x", moves)
    y = lax.axis_index("yh")
    return total[y] + lax.ppermute(total[1 - y], "yh", [(0, 1), (1, 0)])


def shards(tiles, tile_row, tile_col, label_class):
    size = tiles.shape[1]
    near = lax.axis_size(NEAR)
    far = lax.axis_size(FAR)
    rows = lax.axis_size(ROW)
    cols = lax.axis_size(COL)
    chips = lax.axis_size(CHIPS)
    local = tile_row % cols
    mine = local % 2 == lax.axis_index("core")
    source = local // 2 + jnp.where(mine, 0, chips)
    target = tile_col // cols
    label = label_class.reshape(1, size)
    partial_out = shape((rows, CLASSES, size))
    field = shape((CLASSES, size))
    panels_out = shape((chips, CLASSES, size), BF16)
    row_out = shape((1, CLASSES))

    def other_core(own):
        return lax.ppermute(own, "core", [(0, 1), (1, 0)])

    def gather(panels):
        own = exchange(panels, CHIPS)
        return own, other_core(own)

    def everywhere(sums):
        sums = exchange(sums, NEAR)
        return exchange(call(pool_kernel, shape((far, *sums.shape[1:])), sums), FAR)

    labels = exchange(jnp.broadcast_to(label[None], (cols, 1, size)), COL)
    partial, share, count = apply_tiles(
        label_kernel, (partial_out, shape((rows, 1, size)), row_out), (local, target), tiles, labels
    )
    rhs, panels = call(start_kernel, (field, panels_out), exchange(partial, ROW), label)
    own, degree = after(exchange(panels, CHIPS), reduce_by_permutes(share))
    partial, shift = apply_tiles(
        first_panel_kernel, (partial_out, row_out), (source, target), tiles, own, other_core(own), count
    )
    image, panels = call(
        image_kernel, (field, panels_out), exchange(partial, ROW), label, degree, shift, rhs
    )
    partial = apply_tiles(
        shifted_panel_kernel, partial_out, (source, target), tiles, *gather(panels), partial, shift
    )
    second, sums = call(
        second_kernel, (field, shape((near, 1, 7 * CLASSES))),
        exchange(partial, ROW), label, degree, rhs, image,
    )
    solution, residual, direction, panels, norm = call(
        two_steps_kernel, (field, field, field, panels_out, row_out),
        everywhere(sums), rhs, image, second,
    )
    partial = apply_tiles(panel_kernel, partial_out, (source, target), tiles, *gather(panels))
    image, sums = call(
        third_kernel, (field, shape((near * far, 1, CLASSES))),
        exchange(partial, ROW), label, degree, direction,
    )
    out = shape((size, CLASSES))
    return call(
        last_kernel, (out, out), exchange(sums, AXES), norm, solution, residual, direction, image
    )


def solution(mesh):
    torus = Mesh(mesh.devices.reshape(4, 2, 2, 8, 2), AXES)
    return jax.shard_map(
        shards,
        mesh=torus,
        in_specs=(P(AXES, None, None), P(AXES), P(AXES), P(AXES)),
        out_specs=(P(AXES, None), P(AXES, None)),
        check_vma=False,
    )
```
